32 devices in a mesh: row: 4 (over x, core), col: 8 (over z, y).
Axes of the slice: x: 2, y: 2, z: 4, core: 2. Of those that a mesh axis runs over, the one named last changes fastest.
Arguments:
- inputs: bfloat16 [512, 12288], P('col', 'row'), may hold values from -6 to 6
- weight: bfloat16 [12288, 24576], P('row', 'col'), may hold values from -0.0546875 to 0.0546875
- grad_out: bfloat16 [512, 24576], P('row', 'col'), may hold values from -1.2578125 to 1.2578125
Outputs:
- grad_input: bfloat16 [512, 12288], P('col', 'row')
- grad_weight: bfloat16 [12288, 24576], P('row', 'col')
The draws below stay inside these ranges and needn't reach their ends.
All inputs are finite; a program needn't handle non-finite values.
Results may differ from the reference program's by a relative error of at most 0.02.
Values may be sent and summed in bfloat16 or wider, within the bound.
A program may use at most 128 MiB of HBM per device.

```python
import jax
import jax.numpy as jnp
from jax import lax

D = 12288
F = 24576
TOKENS = 512
N_ROW = 4
N_COL = 8


def block_scale(own_key, extent, shards, least, high):
    level, own = 1.0, jax.random.fold_in(own_key, 6)
    for dim, shards_of in shards:
        draws = jnp.exp(jax.random.uniform(jax.random.fold_in(own, dim), (shards_of,), jnp.float32, least / len(shards), high / len(shards)))
        level = level * jnp.repeat(draws, extent[dim] // shards_of).reshape([-1 if axis == dim else 1 for axis in range(len(extent))])
    return level


def gaussian(rng, dims, width, limit, pieces=(), kind=jnp.bfloat16):
    level = block_scale(rng, dims, pieces, -0.22, 0.18) if pieces else 1.0
    array = jax.random.normal(rng, dims, jnp.float32) * width * level
    return jnp.minimum(jnp.maximum(array, -limit), limit).astype(kind)


def setup_inputs(seed: int = 0) -> dict:
    seeds = jax.random.split(jax.random.key(seed), 4)
    inputs = gaussian(seeds[0], (TOKENS, D), 1.0, 6.0, ((0, 8), (1, 4)))
    weight = gaussian(seeds[1], (D, F), D ** -0.5, 0.0546875, ((0, 4), (1, 8)))
    grad_out = gaussian(seeds[2], (TOKENS, F), (TOKENS ** -0.25), 1.2578125, ((0, 4), (1, 8)))
    return {"inputs": inputs, "weight": weight, "grad_out": grad_out}


def gelu_slope(value):
    coef = 0.7978845608
    inner = coef * (value + 0.044715 * value * value * value)
    tanh_val = jnp.tanh(inner)
    return 0.5 * (1.0 + tanh_val) + 0.5 * value * (1.0 - tanh_val * tanh_val) * coef * (1.0 + 3.0 * 0.044715 * value * value)


def reference(inputs, weight, grad_out):
    width_block = D // N_ROW
    unit_block = F // N_COL
    pre = jnp.zeros((inputs.shape[0], weight.shape[1]), jnp.float32)
    for block in range(N_ROW):
        left = inputs[:, block * width_block:(block + 1) * width_block]
        right = weight[block * width_block:(block + 1) * width_block, :]
        partial_sum = jnp.dot(left, right, preferred_element_type=jnp.float32).astype(jnp.bfloat16)
        partial_sum = lax.optimization_barrier(partial_sum)
        pre = pre + partial_sum.astype(jnp.float32)
    grad_pre = (grad_out.astype(jnp.float32) * gelu_slope(pre)).astype(jnp.bfloat16)
    grad_weight = lax.dot_general(inputs, grad_pre, (((0,), (0,)), ((), ())), preferred_element_type=jnp.float32).astype(jnp.bfloat16)
    grad_input = jnp.zeros(inputs.shape, jnp.float32)
    for block in range(N_COL):
        left = grad_pre[:, block * unit_block:(block + 1) * unit_block]
        right = weight[:, block * unit_block:(block + 1) * unit_block]
        term = lax.dot_general(left, right, (((1,), (1,)), ((), ())), preferred_element_type=jnp.float32).astype(jnp.bfloat16)
        term = lax.optimization_barrier(term)
        grad_input = grad_input + term.astype(jnp.float32)
    return grad_input.astype(jnp.bfloat16), grad_weight
```

```python
import functools

import jax
import jax.numpy as jnp
from jax import lax
from jax.experimental import pallas as pl
from jax.experimental.pallas import tpu as pltpu
from jax.sharding import PartitionSpec as P

MESH = pl.DeviceIdType.MESH
PAIR = 2


def gelu_slope(value):
    coef = 0.7978845608
    inner = coef * (value + 0.044715 * value * value * value)
    tanh_val = jnp.tanh(inner)
    return 0.5 * (1.0 + tanh_val) + 0.5 * value * (1.0 - tanh_val * tanh_val) * coef * (
        1.0 + 3.0 * 0.044715 * value * value
    )


def tile_of(width, most):
    tile = 128
    for size in range(128, most + 1, 128):
        if width % size == 0:
            tile = size
    return tile


def block(index, size):
    return pl.ds(pl.multiple_of(index * size, size), size)


def kernel(
    n_row, n_col,
    x_ref, w_ref, go_ref,
    gi_ref, x_out, gp_out,
    w, xs_all, go_all, part, core_in, chip, chip_in, gp, term, pair_in, both, line_in,
    w_sem, x_sem, go_sem, out_sem,
    ag_recv, ag_send, go_recv, go_send, core_recv, core_send, chip_recv, chip_send,
    gp_recv, gp_send, pair_recv, pair_send, line_recv, line_send,
):
    own, depth = x_ref.shape
    units = w_ref.shape[1]
    half = units // PAIR
    line = n_col // PAIR
    chips = n_row // PAIR
    rows = own * PAIR
    held = go_ref.shape[0]
    row, col = lax.axis_index("row"), lax.axis_index("col")
    at, side = col // PAIR, lax.rem(col, PAIR)
    across, core = row // PAIR, lax.rem(row, PAIR)
    mate = (across * PAIR + 1 - core, col)
    twin = (row, at * PAIR + 1 - side)

    def on_line(place):
        return (row, place * PAIR + side)

    def on_chip(place):
        return (place * PAIR + core, col)

    def remote(src, dst, send, recv, device):
        return pltpu.make_async_remote_copy(
            src_ref=src, dst_ref=dst, send_sem=send, recv_sem=recv,
            device_id=device, device_id_type=MESH,
        )

    def chunk_of(k):
        low = jnp.minimum(at, line - 1 - at)
        near = jnp.where(lax.rem(k, 2) == 1, at + (k + 1) // 2, at - (k + 1) // 2)
        far = jnp.where(at < line - 1 - at, at + (k - low), at - (k - low))
        return jnp.where(k <= 2 * low, near, far)

    def slot(q, s):
        return xs_all.at[block(q * PAIR + s, own), :]

    def own_to(which, device):
        return remote(x_ref, slot(at, side), ag_send.at[which, at], ag_recv.at[at, side], device)

    def to_twin(q):
        return remote(slot(q, side), slot(q, side), ag_send.at[0, q], ag_recv.at[q, side], twin)

    def onward(q):
        place = jnp.where(q < at, at + 1, at - 1)
        place = jnp.clip(place, 0, line - 1)
        return remote(slot(q, side), slot(q, side), ag_send.at[1, q], ag_recv.at[q, side], on_line(place))

    def goes_on(q):
        return ((q < at) & (at + 1 < line)) | ((q > at) & (at > 0))

    def arrived(q, s):
        return remote(slot(q, s), slot(q, s), ag_send.at[0, q], ag_recv.at[q, s], twin)

    def go_copy(step):
        other = lax.rem(row + step, n_row)
        return remote(
            go_ref.at[:, block(lax.rem(other, PAIR), half)],
            go_all.at[block(row, held), :],
            go_send.at[step - 1], go_recv.at[row], (other, col),
        )

    def go_arrived(source):
        view = go_all.at[block(source, held), :]
        return remote(view, view, go_send.at[0], go_recv.at[source], mate)

    def core_copy(q):
        return remote(
            part.at[q, :, block(1 - core, half)], core_in.at[q],
            core_send.at[q], core_recv.at[q], mate,
        )

    def chip_copy(q, step):
        place = lax.rem(across + step, chips)
        return remote(
            chip.at[q], chip_in.at[q, across],
            chip_send.at[q, step - 1], chip_recv.at[q, across], on_chip(place),
        )

    def chip_arrived(q, source):
        view = chip_in.at[q, source]
        return remote(view, view, chip_send.at[q, 0], chip_recv.at[q, source], mate)

    def gp_copy(q, which):
        view = gp.at[block(q, rows), block(which, half)]
        return remote(view, view, gp_send.at[q], gp_recv.at[q], mate)

    def pair_copy(q):
        return remote(
            term.at[q, block(1 - side, own), :], pair_in.at[q],
            pair_send.at[q], pair_recv.at[q], twin,
        )

    def line_copy(q):
        return remote(
            both.at[q], line_in.at[at], line_send.at[q], line_recv.at[at], on_line(q)
        )

    def line_arrived(source):
        view = line_in.at[source]
        return remote(view, view, line_send.at[source], line_recv.at[source], twin)

    w_copy = pltpu.make_async_copy(w_ref, w, w_sem)
    x_copy = pltpu.make_async_copy(x_ref, slot(at, side), x_sem)
    go_own = pltpu.make_async_copy(
        go_ref.at[:, block(core, half)], go_all.at[block(row, held), :], go_sem
    )
    w_copy.start()
    x_copy.start()
    go_own.start()

    barrier = pltpu.get_barrier_semaphore()
    pl.semaphore_signal(barrier, inc=1, device_id=twin, device_id_type=MESH)

    @pl.loop(1, line)
    def _(step):
        pl.semaphore_signal(
            barrier, inc=1, device_id=on_line(lax.rem(at + step, line)), device_id_type=MESH
        )

    @pl.loop(1, n_row)
    def _(step):
        pl.semaphore_signal(
            barrier, inc=1, device_id=(lax.rem(row + step, n_row), col), device_id_type=MESH
        )

    pl.semaphore_wait(barrier, line + n_row - 1)

    up, down = jnp.minimum(at + 1, line - 1), jnp.maximum(at - 1, 0)
    own_to(0, twin).start()

    @pl.when(at + 1 < line)
    def _():
        own_to(1, on_line(up)).start()

    @pl.when(at > 0)
    def _():
        own_to(2, on_line(down)).start()

    @pl.loop(1, n_row)
    def _(step):
        go_copy(step).start()

    go_own.wait()

    @pl.loop(1, n_row)
    def _(step):
        go_arrived(lax.rem(row + step, n_row)).wait_recv()

    x_copy.wait()
    w_copy.wait()

    tile = tile_of(half, 512)
    tiles = half // tile
    wide = tile_of(depth, 512)

    def first_product(q, which):
        @pl.loop(0, tiles)
        def _(j):
            columns = block(which * tiles + j, tile)
            part[q, :, columns] = jnp.dot(
                xs_all[block(q, rows), :], w[:, columns], preferred_element_type=jnp.float32
            ).astype(part.dtype)

    small = 16
    span = tile_of(half, 512)

    def slabs(height, width, step, body):
        across_tiles = width // step

        @pl.loop(0, (height // small) * across_tiles)
        def _(i):
            body(lax.div(i, across_tiles) * small, block(lax.rem(i, across_tiles), step))

    @pl.loop(0, line + 2)
    def _(k):
        q = chunk_of(jnp.minimum(k, line - 1))
        before = chunk_of(jnp.clip(k - 1, 0, line - 1))
        earlier = chunk_of(jnp.clip(k - 2, 0, line - 1))

        @pl.when(k + 1 < line)
        def _():
            coming = chunk_of(k + 1)
            arrived(coming, side).wait_recv()
            to_twin(coming).start()

            @pl.when(goes_on(coming))
            def _():
                onward(coming).start()

        @pl.when(k < line)
        def _():
            arrived(q, 1 - side).wait_recv()
            pltpu.make_async_copy(
                xs_all.at[block(q, rows), :], x_out.at[block(q, rows), :], out_sem.at[0, q]
            ).start()
            first_product(q, 1 - core)
            core_copy(q).start()
            first_product(q, core)
            core_copy(q).wait_recv()

            def add(top, columns):
                at_rows = pl.ds(pl.multiple_of(top, small), small)
                mine = part[q, at_rows, pl.ds(pl.multiple_of(core * half, half) + columns.start, span)]
                chip[q, at_rows, columns] = (
                    mine.astype(jnp.float32) + core_in[q, at_rows, columns].astype(jnp.float32)
                ).astype(chip.dtype)

            slabs(rows, half, span, add)

            @pl.loop(1, chips)
            def _(step):
                chip_copy(q, step).start()

        @pl.when((k >= 1) & (k <= line))
        def _():
            @pl.loop(1, chips)
            def _(step):
                chip_arrived(before, lax.rem(across + step, chips)).wait_recv()

            def slope(top, columns):
                at_rows = pl.ds(pl.multiple_of(top, small), small)
                total = chip[before, at_rows, columns].astype(jnp.float32)
                for step in range(1, chips):
                    source = lax.rem(across + step, chips)
                    total = total + chip_in[before, source, at_rows, columns].astype(jnp.float32)
                token = pl.ds(pl.multiple_of(before * rows + top, small), small)
                gp[token, pl.ds(pl.multiple_of(core * half, half) + columns.start, span)] = (
                    go_all[token, columns].astype(jnp.float32) * gelu_slope(total)
                ).astype(gp.dtype)

            slabs(rows, half, span, slope)
            gp_copy(before, core).start()
            gp_copy(before, 1 - core).wait_recv()
            pltpu.make_async_copy(
                gp.at[block(before, rows), :], gp_out.at[block(before, rows), :], out_sem.at[1, before]
            ).start()

            @pl.loop(0, depth // wide)
            def _(j):
                columns = block(j, wide)
                term[before, :, columns] = lax.dot_general(
                    gp[block(before, rows), :], w[columns, :], (((1,), (1,)), ((), ())),
                    preferred_element_type=jnp.float32,
                ).astype(term.dtype)

            pair_copy(before).start()

        @pl.when(k >= 2)
        def _():
            pair_copy(earlier).wait_recv()

            def add(top, columns):
                at_rows = pl.ds(pl.multiple_of(top, small), small)
                mine = term[earlier, pl.ds(pl.multiple_of(side * own + top, small), small), columns]
                both[earlier, at_rows, columns] = (
                    mine.astype(jnp.float32) + pair_in[earlier, at_rows, columns].astype(jnp.float32)
                ).astype(both.dtype)

            slabs(own, depth, wide, add)

            @pl.when(earlier != at)
            def _():
                line_copy(earlier).start()

    @pl.loop(1, line)
    def _(step):
        line_arrived(lax.rem(at + step, line)).wait_recv()

    def finish(top, columns):
        at_rows = pl.ds(pl.multiple_of(top, small), small)
        total = both[at, at_rows, columns].astype(jnp.float32)
        for step in range(1, line):
            total = total + line_in[lax.rem(at + step, line), at_rows, columns].astype(jnp.float32)
        gi_ref[at_rows, columns] = total.astype(gi_ref.dtype)

    slabs(own, depth, wide, finish)

    own_to(0, twin).wait_send()

    @pl.when(at + 1 < line)
    def _():
        own_to(1, on_line(up)).wait_send()

    @pl.when(at > 0)
    def _():
        own_to(2, on_line(down)).wait_send()

    @pl.loop(1, n_row)
    def _(step):
        go_copy(step).wait_send()

    @pl.loop(0, line)
    def _(q):
        @pl.when(q != at)
        def _():
            to_twin(q).wait_send()
            line_copy(q).wait_send()

        @pl.when(goes_on(q))
        def _():
            onward(q).wait_send()

        core_copy(q).wait_send()

        @pl.loop(1, chips)
        def _(step):
            chip_copy(q, step).wait_send()

        gp_copy(q, core).wait_send()
        pair_copy(q).wait_send()
        pltpu.make_async_copy(
            xs_all.at[block(q, rows), :], x_out.at[block(q, rows), :], out_sem.at[0, q]
        ).wait()
        pltpu.make_async_copy(
            gp.at[block(q, rows), :], gp_out.at[block(q, rows), :], out_sem.at[1, q]
        ).wait()


def fused(n_row, n_col, inputs, weight, grad_out):
    own, depth = inputs.shape
    units = weight.shape[1]
    half = units // PAIR
    line, chips = n_col // PAIR, n_row // PAIR
    rows, tokens = own * PAIR, own * n_col
    held = grad_out.shape[0]
    bf16 = jnp.bfloat16
    DMA = pltpu.SemaphoreType.DMA
    flops = 4 * tokens * depth * units
    return pl.pallas_call(
        functools.partial(kernel, n_row, n_col),
        out_shape=(
            jax.ShapeDtypeStruct((own, depth), bf16),
            jax.ShapeDtypeStruct((tokens, depth), bf16),
            jax.ShapeDtypeStruct((tokens, units), bf16),
        ),
        in_specs=[pl.BlockSpec(memory_space=pl.ANY)] * 3,
        out_specs=(
            pl.BlockSpec(memory_space=pltpu.VMEM),
            pl.BlockSpec(memory_space=pl.ANY),
            pl.BlockSpec(memory_space=pl.ANY),
        ),
        scratch_shapes=[
            pltpu.VMEM((depth, units), bf16),
            pltpu.VMEM((tokens, depth), bf16),
            pltpu.VMEM((held * n_row, half), bf16),
            pltpu.VMEM((line, rows, units), bf16),
            pltpu.VMEM((line, rows, half), bf16),
            pltpu.VMEM((line, rows, half), bf16),
            pltpu.VMEM((line, chips, rows, half), bf16),
            pltpu.VMEM((tokens, units), bf16),
            pltpu.VMEM((line, rows, depth), bf16),
            pltpu.VMEM((line, own, depth), bf16),
            pltpu.VMEM((line, own, depth), bf16),
            pltpu.VMEM((line, own, depth), bf16),
            DMA, DMA, DMA, DMA((2, line)),
            DMA((line, PAIR)), DMA((3, line)),
            DMA((n_row,)), DMA((n_row,)),
            DMA((line,)), DMA((line,)),
            DMA((line, chips)), DMA((line, chips)),
            DMA((line,)), DMA((line,)),
            DMA((line,)), DMA((line,)),
            DMA((line,)), DMA((line,)),
        ],
        cost_estimate=pl.CostEstimate(
            flops=flops, bytes_accessed=2 * depth * units, transcendentals=tokens * half
        ),
        compiler_params=pltpu.CompilerParams(
            collective_id=0, has_side_effects=True, vmem_limit_bytes=58 * 1024 * 1024
        ),
    )(inputs, weight, grad_out)


def solution(mesh):
    n_row, n_col = mesh.shape["row"], mesh.shape["col"]

    def shards(inputs, weight, grad_out):
        grad_input, gathered, grad_pre = fused(n_row, n_col, inputs, weight, grad_out)
        grad_weight = lax.dot_general(
            gathered, grad_pre, (((0,), (0,)), ((), ())), preferred_element_type=jnp.float32
        )
        return grad_input, grad_weight.astype(jnp.bfloat16)

    return jax.shard_map(
        shards,
        mesh=mesh,
        in_specs=(P("col", "row"), P("row", "col"), P("row", "col")),
        out_specs=(P("col", "row"), P("row", "col")),
        check_vma=False,
    )
```

```python
import functools

import jax
import jax.numpy as jnp
from jax import lax
from jax.experimental import pallas as pl
from jax.experimental.pallas import tpu as pltpu
from jax.sharding import PartitionSpec as P

MESH = pl.DeviceIdType.MESH
PAIR = 2
TILE = 512
WIDE = 768


def gelu_slope(value):
    coef = 0.7978845608
    inner = coef * (value + 0.044715 * value * value * value)
    tanh_val = jnp.tanh(inner)
    return 0.5 * (1.0 + tanh_val) + 0.5 * value * (1.0 - tanh_val * tanh_val) * coef * (
        1.0 + 3.0 * 0.044715 * value * value
    )


def tile_of(width, most):
    tile = 128
    for size in range(128, most + 1, 128):
        if width % size == 0:
            tile = size
    return tile


def block(index, size):
    return pl.ds(pl.multiple_of(index * size, size), size)


def kernel(
    n_row, n_col,
    x_ref, w_ref, go_ref,
    gi_ref, x_out, gp_out,
    w, xs_all, go_all, part, core_in, chip, chip_in, gp, term, pair_in, both, sib_in, summed, line_in,
    w_sem, x_sem, go_sem, out_sem,
    ag_recv, ag_send, go_recv, go_send, core_recv, core_send, chip_recv, chip_send,
    gp_recv, gp_send, pair_recv, pair_send, sib_recv, sib_send, line_recv, line_send,
):
    own, depth = x_ref.shape
    units = w_ref.shape[1]
    half = units // PAIR
    line = n_col // PAIR
    groups = line // PAIR
    chips = n_row // PAIR
    big = own * PAIR * PAIR
    held = go_ref.shape[0]
    tile, wide = tile_of(half, TILE), tile_of(depth, WIDE)
    tiles, pieces = half // tile, depth // wide
    small = 16
    row, col = lax.axis_index("row"), lax.axis_index("col")
    at, side = lax.div(col, PAIR), lax.rem(col, PAIR)
    group, sib = lax.div(at, PAIR), lax.rem(at, PAIR)
    across, core = lax.div(row, PAIR), lax.rem(row, PAIR)
    mate = (across * PAIR + 1 - core, col)
    twin = (row, at * PAIR + 1 - side)

    def on_line(place):
        return (row, place * PAIR + side)

    def on_chip(place):
        return (place * PAIR + core, col)

    sibling = on_line(group * PAIR + 1 - sib)

    def remote(src, dst, send, recv, device):
        return pltpu.make_async_remote_copy(
            src_ref=src, dst_ref=dst, send_sem=send, recv_sem=recv,
            device_id=device, device_id_type=MESH,
        )

    def group_of(k):
        low = jnp.minimum(group, groups - 1 - group)
        step = lax.div(k + 1, 2)
        near = jnp.where(lax.rem(k, 2) == 1, group + step, group - step)
        far = jnp.where(group < groups - 1 - group, group + (k - low), group - (k - low))
        return jnp.where(k <= 2 * low, near, far)

    def block_of(g, i):
        first = jnp.where(g == group, sib, jnp.where(g > group, 0, 1))
        return g * PAIR + (first if i == 0 else 1 - first)

    def slot(q, s):
        return xs_all.at[block(q * PAIR + s, own), :]

    def own_to(which, device):
        return remote(x_ref, slot(at, side), ag_send.at[which, at], ag_recv.at[at, side], device)

    def to_twin(q):
        return remote(slot(q, side), slot(q, side), ag_send.at[0, q], ag_recv.at[q, side], twin)

    def onward(q):
        place = jnp.clip(jnp.where(q < at, at + 1, at - 1), 0, line - 1)
        return remote(slot(q, side), slot(q, side), ag_send.at[1, q], ag_recv.at[q, side], on_line(place))

    def goes_on(q):
        return ((q < at) & (at + 1 < line)) | ((q > at) & (at > 0))

    def arrived(q, s):
        return remote(slot(q, s), slot(q, s), ag_send.at[0, q], ag_recv.at[q, s], twin)

    def forward(q):
        arrived(q, side).wait_recv()
        to_twin(q).start()

        @pl.when(goes_on(q))
        def _():
            onward(q).start()

    def go_copy(step):
        other = lax.rem(row + step, n_row)
        return remote(
            go_ref.at[:, block(lax.rem(other, PAIR), half)],
            go_all.at[block(row, held), :],
            go_send.at[step - 1], go_recv.at[row], (other, col),
        )

    def go_arrived(source):
        view = go_all.at[block(source, held), :]
        return remote(view, view, go_send.at[0], go_recv.at[source], mate)

    def core_copy(g, j):
        return remote(
            part.at[g, :, block((1 - core) * tiles + j, tile)], core_in.at[g, :, block(j, tile)],
            core_send.at[g, j], core_recv.at[g, j], mate,
        )

    def chip_copy(g, step, j):
        place = lax.rem(across + step, chips)
        return remote(
            chip.at[g, :, block(j, tile)], chip_in.at[g, across, :, block(j, tile)],
            chip_send.at[g, step - 1, j], chip_recv.at[g, across, j], on_chip(place),
        )

    def chip_arrived(g, source, j):
        view = chip_in.at[g, source, :, block(j, tile)]
        return remote(view, view, chip_send.at[g, 0, j], chip_recv.at[g, source, j], mate)

    def gp_copy(g, which, j):
        view = gp.at[block(g, big), block(which * tiles + j, tile)]
        return remote(view, view, gp_send.at[g, j], gp_recv.at[g, j], mate)

    def pair_copy(g, b, j):
        return remote(
            term.at[g, block(b * PAIR + 1 - side, own), block(j, wide)],
            pair_in.at[g, block(b, own), block(j, wide)],
            pair_send.at[g, b, j], pair_recv.at[g, b, j], twin,
        )

    def sib_copy(g, j):
        return remote(
            both.at[g, block(1 - sib, own), block(j, wide)], sib_in.at[g, :, block(j, wide)],
            sib_send.at[g, j], sib_recv.at[g, j], sibling,
        )

    def line_copy(g, j):
        return remote(
            summed.at[g, :, block(j, wide)], line_in.at[group, :, block(j, wide)],
            line_send.at[g, j], line_recv.at[group, j], on_line(g * PAIR + sib),
        )

    def line_arrived(source, j):
        view = line_in.at[source, :, block(j, wide)]
        return remote(view, view, line_send.at[source, j], line_recv.at[source, j], twin)

    def x_copy_out(g):
        return pltpu.make_async_copy(
            xs_all.at[block(g, big), :], x_out.at[block(g, big), :], out_sem.at[0, g]
        )

    def gp_copy_out(g):
        return pltpu.make_async_copy(
            gp.at[block(g, big), :], gp_out.at[block(g, big), :], out_sem.at[1, g]
        )

    w_copy = pltpu.make_async_copy(w_ref, w, w_sem)
    x_copy = pltpu.make_async_copy(x_ref, slot(at, side), x_sem)
    go_own = pltpu.make_async_copy(
        go_ref.at[:, block(core, half)], go_all.at[block(row, held), :], go_sem
    )
    x_copy.start()
    go_own.start()
    w_copy.start()

    barrier = pltpu.get_barrier_semaphore()
    pl.semaphore_signal(barrier, inc=1, device_id=twin, device_id_type=MESH)

    @pl.loop(1, line)
    def _(step):
        pl.semaphore_signal(
            barrier, inc=1, device_id=on_line(lax.rem(at + step, line)), device_id_type=MESH
        )

    @pl.loop(1, n_row)
    def _(step):
        pl.semaphore_signal(
            barrier, inc=1, device_id=(lax.rem(row + step, n_row), col), device_id_type=MESH
        )

    pl.semaphore_wait(barrier, line + n_row - 1)

    up, down = jnp.minimum(at + 1, line - 1), jnp.maximum(at - 1, 0)
    own_to(0, twin).start()

    @pl.when(at + 1 < line)
    def _():
        own_to(1, on_line(up)).start()

    @pl.when(at > 0)
    def _():
        own_to(2, on_line(down)).start()

    @pl.loop(1, n_row)
    def _(step):
        go_copy(step).start()

    x_copy.wait()
    forward(block_of(group, 1))

    def slabs(height, base, width, body):
        @pl.loop(0, height // small)
        def _(i):
            body(pl.multiple_of(i * small, small), pl.ds(pl.multiple_of(base * width, width), width))

    def at_row(start):
        return pl.ds(pl.multiple_of(start, small), small)

    def product(g, which):
        columns = block(which, tile)
        part[g, :, columns] = jnp.dot(
            xs_all[block(g, big), :], w[:, columns], preferred_element_type=jnp.float32
        ).astype(part.dtype)

    @pl.loop(0, groups + 3)
    def _(k):
        g = group_of(jnp.minimum(k, groups - 1))
        g1 = group_of(jnp.clip(k - 1, 0, groups - 1))
        g2 = group_of(jnp.clip(k - 2, 0, groups - 1))
        g3 = group_of(jnp.clip(k - 3, 0, groups - 1))
        coming = group_of(jnp.minimum(k + 1, groups - 1))
        more = k + 1 < groups
        second = block_of(coming, 1)

        @pl.when(more)
        def _():
            forward(block_of(coming, 0))

        @pl.when(k < groups)
        def _():
            for i in range(PAIR):
                arrived(block_of(g, i), 1 - side).wait_recv()
            x_copy_out(g).start()

            @pl.when(k == 0)
            def _():
                w_copy.wait()

            @pl.loop(0, tiles)
            def _(j):
                product(g, (1 - core) * tiles + j)
                core_copy(g, j).start()
                product(g, core * tiles + j)

                @pl.when(more & (j == tiles // 2) & goes_on(second))
                def _():
                    forward(second)

                core_copy(g, j).wait_recv()

                def add(top, columns):
                    mine = part[g, at_row(top), block(core * tiles + j, tile)]
                    chip[g, at_row(top), columns] = (
                        mine.astype(jnp.float32)
                        + core_in[g, at_row(top), columns].astype(jnp.float32)
                    ).astype(chip.dtype)

                slabs(big, j, tile, add)

                @pl.loop(1, chips)
                def _(step):
                    chip_copy(g, step, j).start()

            @pl.when(more & ~goes_on(second))
            def _():
                forward(second)

        @pl.when((k >= 1) & (k <= groups))
        def _():
            @pl.when(k == 1)
            def _():
                go_own.wait()

                @pl.loop(1, n_row)
                def _(step):
                    go_arrived(lax.rem(row + step, n_row)).wait_recv()

            @pl.loop(0, tiles)
            def _(j):
                @pl.loop(1, chips)
                def _(step):
                    chip_arrived(g1, lax.rem(across + step, chips), j).wait_recv()

                def slope(top, columns):
                    total = chip[g1, at_row(top), columns].astype(jnp.float32)
                    for step in range(1, chips):
                        source = lax.rem(across + step, chips)
                        total = total + chip_in[g1, source, at_row(top), columns].astype(jnp.float32)
                    token = at_row(g1 * big + top)
                    gp[token, block(core * tiles + j, tile)] = (
                        go_all[token, columns].astype(jnp.float32) * gelu_slope(total)
                    ).astype(gp.dtype)

                slabs(big, j, tile, slope)
                gp_copy(g1, core, j).start()

            @pl.loop(0, tiles)
            def _(j):
                gp_copy(g1, 1 - core, j).wait_recv()

            gp_copy_out(g1).start()

            @pl.loop(0, pieces)
            def _(j):
                columns = block(j, wide)
                term[g1, :, columns] = lax.dot_general(
                    gp[block(g1, big), :], w[columns, :], (((1,), (1,)), ((), ())),
                    preferred_element_type=jnp.float32,
                ).astype(term.dtype)
                for b in range(PAIR):
                    pair_copy(g1, b, j).start()

        @pl.when((k >= 2) & (k <= groups + 1))
        def _():
            @pl.loop(0, pieces)
            def _(j):
                for b in range(PAIR):
                    pair_copy(g2, b, j).wait_recv()

                    def add(top, columns):
                        mine = term[g2, at_row((b * PAIR + side) * own + top), columns]
                        here = at_row(b * own + top)
                        both[g2, here, columns] = (
                            mine.astype(jnp.float32)
                            + pair_in[g2, here, columns].astype(jnp.float32)
                        ).astype(both.dtype)

                    slabs(own, j, wide, add)
                sib_copy(g2, j).start()

        @pl.when(k >= 3)
        def _():
            @pl.loop(0, pieces)
            def _(j):
                sib_copy(g3, j).wait_recv()

                def add(top, columns):
                    mine = both[g3, at_row(sib * own + top), columns]
                    summed[g3, at_row(top), columns] = (
                        mine.astype(jnp.float32)
                        + sib_in[g3, at_row(top), columns].astype(jnp.float32)
                    ).astype(summed.dtype)

                slabs(own, j, wide, add)

                @pl.when(g3 != group)
                def _():
                    line_copy(g3, j).start()

    @pl.loop(0, pieces)
    def _(j):
        @pl.loop(1, groups)
        def _(step):
            line_arrived(lax.rem(group + step, groups), j).wait_recv()

        def finish(top, columns):
            total = summed[group, at_row(top), columns].astype(jnp.float32)
            for step in range(1, groups):
                source = lax.rem(group + step, groups)
                total = total + line_in[source, at_row(top), columns].astype(jnp.float32)
            gi_ref[at_row(top), columns] = total.astype(gi_ref.dtype)

        slabs(own, j, wide, finish)

    own_to(0, twin).wait_send()

    @pl.when(at + 1 < line)
    def _():
        own_to(1, on_line(up)).wait_send()

    @pl.when(at > 0)
    def _():
        own_to(2, on_line(down)).wait_send()

    @pl.loop(1, n_row)
    def _(step):
        go_copy(step).wait_send()

    @pl.loop(0, line)
    def _(q):
        @pl.when(q != at)
        def _():
            to_twin(q).wait_send()

        @pl.when(goes_on(q))
        def _():
            onward(q).wait_send()

    @pl.loop(0, groups)
    def _(g):
        @pl.loop(0, tiles)
        def _(j):
            core_copy(g, j).wait_send()

            @pl.loop(1, chips)
            def _(step):
                chip_copy(g, step, j).wait_send()

            gp_copy(g, core, j).wait_send()

        @pl.loop(0, pieces)
        def _(j):
            for b in range(PAIR):
                pair_copy(g, b, j).wait_send()
            sib_copy(g, j).wait_send()

            @pl.when(g != group)
            def _():
                line_copy(g, j).wait_send()

        x_copy_out(g).wait()
        gp_copy_out(g).wait()


def fused(n_row, n_col, inputs, weight, grad_out):
    own, depth = inputs.shape
    units = weight.shape[1]
    half = units // PAIR
    line, chips = n_col // PAIR, n_row // PAIR
    groups = line // PAIR
    big, tokens = own * PAIR * PAIR, own * n_col
    tiles, pieces = half // tile_of(half, TILE), depth // tile_of(depth, WIDE)
    held = grad_out.shape[0]
    bf16 = jnp.bfloat16
    DMA = pltpu.SemaphoreType.DMA
    flops = 4 * tokens * depth * units
    return pl.pallas_call(
        functools.partial(kernel, n_row, n_col),
        out_shape=(
            jax.ShapeDtypeStruct((own, depth), bf16),
            jax.ShapeDtypeStruct((tokens, depth), bf16),
            jax.ShapeDtypeStruct((tokens, units), bf16),
        ),
        in_specs=[pl.BlockSpec(memory_space=pl.ANY)] * 3,
        out_specs=(
            pl.BlockSpec(memory_space=pltpu.VMEM),
            pl.BlockSpec(memory_space=pl.ANY),
            pl.BlockSpec(memory_space=pl.ANY),
        ),
        scratch_shapes=[
            pltpu.VMEM((depth, units), bf16),
            pltpu.VMEM((tokens, depth), bf16),
            pltpu.VMEM((held * n_row, half), bf16),
            pltpu.VMEM((groups, big, units), bf16),
            pltpu.VMEM((groups, big, half), bf16),
            pltpu.VMEM((groups, big, half), bf16),
            pltpu.VMEM((groups, chips, big, half), bf16),
            pltpu.VMEM((tokens, units), bf16),
            pltpu.VMEM((groups, big, depth), bf16),
            pltpu.VMEM((groups, own * PAIR, depth), bf16),
            pltpu.VMEM((groups, own * PAIR, depth), bf16),
            pltpu.VMEM((groups, own, depth), bf16),
            pltpu.VMEM((groups, own, depth), bf16),
            pltpu.VMEM((groups, own, depth), bf16),
            DMA, DMA, DMA, DMA((2, groups)),
            DMA((line, PAIR)), DMA((3, line)),
            DMA((n_row,)), DMA((n_row,)),
            DMA((groups, tiles)), DMA((groups, tiles)),
            DMA((groups, chips, tiles)), DMA((groups, chips, tiles)),
            DMA((groups, tiles)), DMA((groups, tiles)),
            DMA((groups, PAIR, pieces)), DMA((groups, PAIR, pieces)),
            DMA((groups, pieces)), DMA((groups, pieces)),
            DMA((groups, pieces)), DMA((groups, pieces)),
        ],
        cost_estimate=pl.CostEstimate(
            flops=flops, bytes_accessed=2 * depth * units, transcendentals=tokens * half
        ),
        compiler_params=pltpu.CompilerParams(
            collective_id=0, has_side_effects=True, vmem_limit_bytes=58 * 1024 * 1024
        ),
    )(inputs, weight, grad_out)


def solution(mesh):
    n_row, n_col = mesh.shape["row"], mesh.shape["col"]

    def shards(inputs, weight, grad_out):
        grad_input, gathered, grad_pre = fused(n_row, n_col, inputs, weight, grad_out)
        grad_weight = lax.dot_general(
            gathered, grad_pre, (((0,), (0,)), ((), ())), preferred_element_type=jnp.float32
        )
        return grad_input, grad_weight.astype(jnp.bfloat16)

    return jax.shard_map(
        shards,
        mesh=mesh,
        in_specs=(P("col", "row"), P("row", "col"), P("row", "col")),
        out_specs=(P("col", "row"), P("row", "col")),
        check_vma=False,
    )
```

```python
import functools

import jax
import jax.numpy as jnp
from jax import lax
from jax.experimental import pallas as pl
from jax.experimental.pallas import tpu as pltpu
from jax.sharding import PartitionSpec as P

MESH = pl.DeviceIdType.MESH
PAIR = 2
TILE = 512
WIDE = 768


def gelu_slope(value):
    coef = 0.7978845608
    inner = coef * (value + 0.044715 * value * value * value)
    tanh_val = jnp.tanh(inner)
    return 0.5 * (1.0 + tanh_val) + 0.5 * value * (1.0 - tanh_val * tanh_val) * coef * (
        1.0 + 3.0 * 0.044715 * value * value
    )


def tile_of(width, most):
    tile = 128
    for size in range(128, most + 1, 128):
        if width % size == 0:
            tile = size
    return tile


def block(index, size):
    return pl.ds(pl.multiple_of(index * size, size), size)


def kernel(
    n_row, n_col,
    x_ref, w_ref, go_ref,
    gi_ref, x_out, gp_out,
    w, xs_all, go_all, part, core_in, chip, chip_in, gp, term, pair_in, both, sib_in, summed, line_in,
    w_sem, x_sem, go_sem, out_sem,
    z_recv, z_send, y_recv, y_send, go_recv, go_send, core_recv, core_send, chip_recv, chip_send,
    gp_recv, gp_send, pair_recv, pair_send, sib_recv, sib_send, line_recv, line_send,
):
    own, depth = x_ref.shape
    units = w_ref.shape[1]
    half = units // PAIR
    line = n_col // PAIR
    groups = line // PAIR
    chips = n_row // PAIR
    big = own * PAIR * PAIR
    held = go_ref.shape[0]
    tile, wide = tile_of(half, TILE), tile_of(depth, WIDE)
    tiles, pieces = half // tile, depth // wide
    small = 16
    row, col = lax.axis_index("row"), lax.axis_index("col")
    at, side = lax.div(col, PAIR), lax.rem(col, PAIR)
    group, sib = lax.div(at, PAIR), lax.rem(at, PAIR)
    across, core = lax.div(row, PAIR), lax.rem(row, PAIR)
    mate = (across * PAIR + 1 - core, col)
    twin = (row, at * PAIR + 1 - side)

    def on_line(place):
        return (row, place * PAIR + side)

    def on_chip(place):
        return (place * PAIR + core, col)

    beside = group * PAIR + 1 - sib
    sibling = on_line(beside)

    def remote(src, dst, send, recv, device):
        return pltpu.make_async_remote_copy(
            src_ref=src, dst_ref=dst, send_sem=send, recv_sem=recv,
            device_id=device, device_id_type=MESH,
        )

    def group_of(k):
        low = jnp.minimum(group, groups - 1 - group)
        step = lax.div(k + 1, 2)
        near = jnp.where(lax.rem(k, 2) == 1, group + step, group - step)
        far = jnp.where(group < groups - 1 - group, group + (k - low), group - (k - low))
        return jnp.where(k <= 2 * low, near, far)

    def block_of(g, i):
        first = jnp.where(g == group, sib, jnp.where(g > group, 0, 1))
        return g * PAIR + (first if i == 0 else 1 - first)

    def slot(q, s):
        return xs_all.at[block(q * PAIR + s, own), :]

    def slot_half(q, s, h):
        return xs_all.at[block((q * PAIR + s) * 2 + h, own // 2), :]

    def own_to(which, device):
        return remote(x_ref, slot(at, side), z_send.at[which, at], z_recv.at[at], device)

    def own_half(h):
        return remote(
            x_ref.at[block(h, own // 2), :], slot_half(at, side, h),
            y_send.at[at, h], y_recv.at[at, h], twin,
        )

    def to_twin(q, h):
        view = slot_half(q, side, h)
        return remote(view, view, y_send.at[q, h], y_recv.at[q, h], twin)

    def twin_to_sibling():
        view = slot_half(at, 1 - side, 1)
        return remote(view, view, y_send.at[beside, 1], y_recv.at[at, 1], sibling)

    def onward(q):
        place = jnp.clip(jnp.where(q < at, at + 1, at - 1), 0, line - 1)
        return remote(slot(q, side), slot(q, side), z_send.at[1, q], z_recv.at[q], on_line(place))

    def goes_on(q):
        return ((q < at) & (at + 1 < line)) | ((q > at) & (at > 0))

    def wait_z(q):
        remote(slot(q, side), slot(q, side), z_send.at[1, q], z_recv.at[q], twin).wait_recv()

    def wait_y(q, h):
        view = slot_half(q, 1 - side, h)
        remote(view, view, y_send.at[q, h], y_recv.at[q, h], twin).wait_recv()

    def go_copy(step):
        other = lax.rem(row + step, n_row)
        return remote(
            go_ref.at[:, block(lax.rem(other, PAIR), half)],
            go_all.at[block(row, held), :],
            go_send.at[step - 1], go_recv.at[row], (other, col),
        )

    def go_arrived(source):
        view = go_all.at[block(source, held), :]
        return remote(view, view, go_send.at[0], go_recv.at[source], mate)

    def core_copy(g, j):
        return remote(
            part.at[g, :, block((1 - core) * tiles + j, tile)], core_in.at[g, :, block(j, tile)],
            core_send.at[g, j], core_recv.at[g, j], mate,
        )

    def chip_copy(g, step, j):
        place = lax.rem(across + step, chips)
        return remote(
            chip.at[g, :, block(j, tile)], chip_in.at[g, across, :, block(j, tile)],
            chip_send.at[g, step - 1, j], chip_recv.at[g, across, j], on_chip(place),
        )

    def chip_arrived(g, source, j):
        view = chip_in.at[g, source, :, block(j, tile)]
        return remote(view, view, chip_send.at[g, 0, j], chip_recv.at[g, source, j], mate)

    def gp_copy(g, which, j):
        view = gp.at[block(g, big), block(which * tiles + j, tile)]
        return remote(view, view, gp_send.at[g, j], gp_recv.at[g, j], mate)

    def swapped(j):
        return lax.rem(j, 4) == 0

    def by(j, kept, other):
        return jnp.where(swapped(j), other, kept)

    beside_col, twin_col = beside * PAIR + side, at * PAIR + 1 - side

    def pair_copy(g, b, j):
        source = by(j, b * PAIR + 1 - side, (1 - sib) * PAIR + b)
        return remote(
            term.at[g, block(source, own), block(j, wide)],
            pair_in.at[g, block(b, own), block(j, wide)],
            pair_send.at[g, b, j], pair_recv.at[g, b, j], (row, by(j, twin_col, beside_col)),
        )

    def sib_copy(g, j):
        source = by(j, 1 - sib, 1 - side)
        return remote(
            both.at[g, block(source, own), block(j, wide)], sib_in.at[g, :, block(j, wide)],
            sib_send.at[g, j], sib_recv.at[g, j], (row, by(j, beside_col, twin_col)),
        )

    def line_copy(g, j):
        return remote(
            summed.at[g, :, block(j, wide)], line_in.at[group, :, block(j, wide)],
            line_send.at[g, j], line_recv.at[group, j], on_line(g * PAIR + sib),
        )

    def line_arrived(source, j):
        view = line_in.at[source, :, block(j, wide)]
        return remote(view, view, line_send.at[source, j], line_recv.at[source, j], twin)

    def x_copy_out(g):
        return pltpu.make_async_copy(
            xs_all.at[block(g, big), :], x_out.at[block(g, big), :], out_sem.at[0, g]
        )

    def gp_copy_out(g):
        return pltpu.make_async_copy(
            gp.at[block(g, big), :], gp_out.at[block(g, big), :], out_sem.at[1, g]
        )

    w_copy = pltpu.make_async_copy(w_ref, w, w_sem)
    x_copy = pltpu.make_async_copy(x_ref, slot(at, side), x_sem)
    go_own = pltpu.make_async_copy(
        go_ref.at[:, block(core, half)], go_all.at[block(row, held), :], go_sem
    )
    x_copy.start()
    go_own.start()
    w_copy.start()

    barrier = pltpu.get_barrier_semaphore()
    pl.semaphore_signal(barrier, inc=1, device_id=twin, device_id_type=MESH)

    @pl.loop(1, line)
    def _(step):
        pl.semaphore_signal(
            barrier, inc=1, device_id=on_line(lax.rem(at + step, line)), device_id_type=MESH
        )

    @pl.loop(1, n_row)
    def _(step):
        pl.semaphore_signal(
            barrier, inc=1, device_id=(lax.rem(row + step, n_row), col), device_id_type=MESH
        )

    pl.semaphore_wait(barrier, line + n_row - 1)

    up, down = jnp.minimum(at + 1, line - 1), jnp.maximum(at - 1, 0)
    own_half(1).start()

    @pl.when(at + 1 < line)
    def _():
        own_to(1, on_line(up)).start()

    @pl.when(at > 0)
    def _():
        own_to(2, on_line(down)).start()

    own_half(0).start()

    @pl.loop(1, n_row)
    def _(step):
        go_copy(step).start()

    x_copy.wait()
    wait_y(at, 1)
    twin_to_sibling().start()
    wait_z(beside)
    to_twin(beside, 0).start()

    @pl.when(goes_on(beside))
    def _():
        onward(beside).start()

    wait_y(at, 0)

    def slabs(height, base, width, body):
        @pl.loop(0, height // small)
        def _(i):
            body(pl.multiple_of(i * small, small), pl.ds(pl.multiple_of(base * width, width), width))

    def at_row(start):
        return pl.ds(pl.multiple_of(start, small), small)

    def product(g, which):
        columns = block(which, tile)
        part[g, :, columns] = jnp.dot(
            xs_all[block(g, big), :], w[:, columns], preferred_element_type=jnp.float32
        ).astype(part.dtype)

    @pl.loop(0, groups + 3)
    def _(k):
        g = group_of(jnp.minimum(k, groups - 1))
        g1 = group_of(jnp.clip(k - 1, 0, groups - 1))
        g2 = group_of(jnp.clip(k - 2, 0, groups - 1))
        g3 = group_of(jnp.clip(k - 3, 0, groups - 1))
        coming = group_of(jnp.minimum(k + 1, groups - 1))
        more = k + 1 < groups
        first, second = block_of(coming, 0), block_of(coming, 1)

        @pl.when(more & goes_on(first))
        def _():
            wait_z(first)
            onward(first).start()

        @pl.when(k < groups)
        def _():
            for i in range(PAIR):
                @pl.when((k > 0) | (block_of(g, i) != at))
                def _():
                    for h in range(2):
                        wait_y(block_of(g, i), h)

            @pl.when(more & goes_on(first))
            def _():
                for h in range(2):
                    to_twin(first, h).start()

            x_copy_out(g).start()

            @pl.when(k == 0)
            def _():
                w_copy.wait()

            @pl.loop(0, tiles)
            def _(j):
                product(g, (1 - core) * tiles + j)
                core_copy(g, j).start()
                product(g, core * tiles + j)

                @pl.when(more & (j == 0) & ~goes_on(first))
                def _():
                    wait_z(first)
                    for h in range(2):
                        to_twin(first, h).start()

                @pl.when(more & (j == tiles // 2) & goes_on(second))
                def _():
                    wait_z(second)
                    onward(second).start()
                    for h in range(2):
                        to_twin(second, h).start()

                core_copy(g, j).wait_recv()

                def add(top, columns):
                    mine = part[g, at_row(top), block(core * tiles + j, tile)]
                    chip[g, at_row(top), columns] = (
                        mine.astype(jnp.float32)
                        + core_in[g, at_row(top), columns].astype(jnp.float32)
                    ).astype(chip.dtype)

                slabs(big, j, tile, add)

                @pl.loop(1, chips)
                def _(step):
                    chip_copy(g, step, j).start()

            @pl.when(more & ~goes_on(second))
            def _():
                wait_z(second)
                for h in range(2):
                    to_twin(second, h).start()

        @pl.when((k >= 1) & (k <= groups))
        def _():
            @pl.when(k == 1)
            def _():
                go_own.wait()

                @pl.loop(1, n_row)
                def _(step):
                    go_arrived(lax.rem(row + step, n_row)).wait_recv()

            @pl.loop(0, tiles)
            def _(j):
                @pl.loop(1, chips)
                def _(step):
                    chip_arrived(g1, lax.rem(across + step, chips), j).wait_recv()

                def slope(top, columns):
                    total = chip[g1, at_row(top), columns].astype(jnp.float32)
                    for step in range(1, chips):
                        source = lax.rem(across + step, chips)
                        total = total + chip_in[g1, source, at_row(top), columns].astype(jnp.float32)
                    token = at_row(g1 * big + top)
                    gp[token, block(core * tiles + j, tile)] = (
                        go_all[token, columns].astype(jnp.float32) * gelu_slope(total)
                    ).astype(gp.dtype)

                slabs(big, j, tile, slope)
                gp_copy(g1, core, j).start()

            @pl.loop(0, tiles)
            def _(j):
                gp_copy(g1, 1 - core, j).wait_recv()

            gp_copy_out(g1).start()

            @pl.loop(0, pieces)
            def _(j):
                columns = block(j, wide)
                term[g1, :, columns] = lax.dot_general(
                    gp[block(g1, big), :], w[columns, :], (((1,), (1,)), ((), ())),
                    preferred_element_type=jnp.float32,
                ).astype(term.dtype)
                for b in range(PAIR):
                    pair_copy(g1, b, j).start()

        @pl.when((k >= 2) & (k <= groups + 1))
        def _():
            @pl.loop(0, pieces)
            def _(j):
                for b in range(PAIR):
                    pair_copy(g2, b, j).wait_recv()

                    def add(top, columns):
                        mine = term[g2, at_row(by(j, b * PAIR + side, sib * PAIR + b) * own + top), columns]
                        here = at_row(b * own + top)
                        both[g2, here, columns] = (
                            mine.astype(jnp.float32)
                            + pair_in[g2, here, columns].astype(jnp.float32)
                        ).astype(both.dtype)

                    slabs(own, j, wide, add)
                sib_copy(g2, j).start()

        @pl.when(k >= 3)
        def _():
            @pl.loop(0, pieces)
            def _(j):
                sib_copy(g3, j).wait_recv()

                def add(top, columns):
                    mine = both[g3, at_row(by(j, sib, side) * own + top), columns]
                    summed[g3, at_row(top), columns] = (
                        mine.astype(jnp.float32)
                        + sib_in[g3, at_row(top), columns].astype(jnp.float32)
                    ).astype(summed.dtype)

                slabs(own, j, wide, add)

                @pl.when(g3 != group)
                def _():
                    line_copy(g3, j).start()

    @pl.loop(0, pieces)
    def _(j):
        @pl.loop(1, groups)
        def _(step):
            line_arrived(lax.rem(group + step, groups), j).wait_recv()

        def finish(top, columns):
            total = summed[group, at_row(top), columns].astype(jnp.float32)
            for step in range(1, groups):
                source = lax.rem(group + step, groups)
                total = total + line_in[source, at_row(top), columns].astype(jnp.float32)
            gi_ref[at_row(top), columns] = total.astype(gi_ref.dtype)

        slabs(own, j, wide, finish)

    own_half(0).wait_send()
    own_half(1).wait_send()
    twin_to_sibling().wait_send()

    @pl.when(at + 1 < line)
    def _():
        own_to(1, on_line(up)).wait_send()

    @pl.when(at > 0)
    def _():
        own_to(2, on_line(down)).wait_send()

    @pl.loop(1, n_row)
    def _(step):
        go_copy(step).wait_send()

    @pl.loop(0, line)
    def _(q):
        @pl.when(q != at)
        def _():
            to_twin(q, 0).wait_send()

        @pl.when((q != at) & (q != beside))
        def _():
            to_twin(q, 1).wait_send()

        @pl.when(goes_on(q))
        def _():
            onward(q).wait_send()

    @pl.loop(0, groups)
    def _(g):
        @pl.loop(0, tiles)
        def _(j):
            core_copy(g, j).wait_send()

            @pl.loop(1, chips)
            def _(step):
                chip_copy(g, step, j).wait_send()

            gp_copy(g, core, j).wait_send()

        @pl.loop(0, pieces)
        def _(j):
            for b in range(PAIR):
                pair_copy(g, b, j).wait_send()
            sib_copy(g, j).wait_send()

            @pl.when(g != group)
            def _():
                line_copy(g, j).wait_send()

        x_copy_out(g).wait()
        gp_copy_out(g).wait()


def fused(n_row, n_col, inputs, weight, grad_out):
    own, depth = inputs.shape
    units = weight.shape[1]
    half = units // PAIR
    line, chips = n_col // PAIR, n_row // PAIR
    groups = line // PAIR
    big, tokens = own * PAIR * PAIR, own * n_col
    tiles, pieces = half // tile_of(half, TILE), depth // tile_of(depth, WIDE)
    held = grad_out.shape[0]
    bf16 = jnp.bfloat16
    DMA = pltpu.SemaphoreType.DMA
    flops = 4 * tokens * depth * units
    return pl.pallas_call(
        functools.partial(kernel, n_row, n_col),
        out_shape=(
            jax.ShapeDtypeStruct((own, depth), bf16),
            jax.ShapeDtypeStruct((tokens, depth), bf16),
            jax.ShapeDtypeStruct((tokens, units), bf16),
        ),
        in_specs=[pl.BlockSpec(memory_space=pl.ANY)] * 3,
        out_specs=(
            pl.BlockSpec(memory_space=pltpu.VMEM),
            pl.BlockSpec(memory_space=pl.ANY),
            pl.BlockSpec(memory_space=pl.ANY),
        ),
        scratch_shapes=[
            pltpu.VMEM((depth, units), bf16),
            pltpu.VMEM((tokens, depth), bf16),
            pltpu.VMEM((held * n_row, half), bf16),
            pltpu.VMEM((groups, big, units), bf16),
            pltpu.VMEM((groups, big, half), bf16),
            pltpu.VMEM((groups, big, half), bf16),
            pltpu.VMEM((groups, chips, big, half), bf16),
            pltpu.VMEM((tokens, units), bf16),
            pltpu.VMEM((groups, big, depth), bf16),
            pltpu.VMEM((groups, own * PAIR, depth), bf16),
            pltpu.VMEM((groups, own * PAIR, depth), bf16),
            pltpu.VMEM((groups, own, depth), bf16),
            pltpu.VMEM((groups, own, depth), bf16),
            pltpu.VMEM((groups, own, depth), bf16),
            DMA, DMA, DMA, DMA((2, groups)),
            DMA((line,)), DMA((3, line)), DMA((line, 2)), DMA((line, 2)),
            DMA((n_row,)), DMA((n_row,)),
            DMA((groups, tiles)), DMA((groups, tiles)),
            DMA((groups, chips, tiles)), DMA((groups, chips, tiles)),
            DMA((groups, tiles)), DMA((groups, tiles)),
            DMA((groups, PAIR, pieces)), DMA((groups, PAIR, pieces)),
            DMA((groups, pieces)), DMA((groups, pieces)),
            DMA((groups, pieces)), DMA((groups, pieces)),
        ],
        cost_estimate=pl.CostEstimate(
            flops=flops, bytes_accessed=2 * depth * units, transcendentals=tokens * half
        ),
        compiler_params=pltpu.CompilerParams(
            collective_id=0, has_side_effects=True, vmem_limit_bytes=58 * 1024 * 1024
        ),
    )(inputs, weight, grad_out)


def solution(mesh):
    n_row, n_col = mesh.shape["row"], mesh.shape["col"]

    def shards(inputs, weight, grad_out):
        grad_input, gathered, grad_pre = fused(n_row, n_col, inputs, weight, grad_out)
        grad_weight = lax.dot_general(
            gathered, grad_pre, (((0,), (0,)), ((), ())), preferred_element_type=jnp.float32
        )
        return grad_input, grad_weight.astype(jnp.bfloat16)

    return jax.shard_map(
        shards,
        mesh=mesh,
        in_specs=(P("col", "row"), P("row", "col"), P("row", "col")),
        out_specs=(P("col", "row"), P("row", "col")),
        check_vma=False,
    )
```

```python
import functools

import jax
import jax.numpy as jnp
from jax import lax
from jax.experimental import pallas as pl
from jax.experimental.pallas import tpu as pltpu
from jax.sharding import PartitionSpec as P

MESH = pl.DeviceIdType.MESH
PAIR = 2
TILE = 512
WIDE = 768


def gelu_slope(value):
    coef = 0.7978845608
    inner = coef * (value + 0.044715 * value * value * value)
    tanh_val = jnp.tanh(inner)
    return 0.5 * (1.0 + tanh_val) + 0.5 * value * (1.0 - tanh_val * tanh_val) * coef * (
        1.0 + 3.0 * 0.044715 * value * value
    )


def tile_of(width, most):
    tile = 128
    for size in range(128, most + 1, 128):
        if width % size == 0:
            tile = size
    return tile


def block(index, size):
    return pl.ds(pl.multiple_of(index * size, size), size)


def kernel(
    n_row, n_col,
    x_ref, w_ref, go_ref,
    gi_ref, x_out, gp_out,
    w, xs_all, go_all, part, core_in, chip, chip_in, gp, term, pair_in, both, sib_in, summed, line_in,
    w_sem, x_sem, go_sem, out_sem,
    z_recv, z_send, y_recv, y_send, go_recv, go_send, core_recv, core_send, chip_recv, chip_send,
    gp_recv, gp_send, pair_recv, pair_send, sib_recv, sib_send, line_recv, line_send,
):
    own, depth = x_ref.shape
    units = w_ref.shape[1]
    half = units // PAIR
    line = n_col // PAIR
    groups = line // PAIR
    chips = n_row // PAIR
    big = own * PAIR * PAIR
    held = go_ref.shape[0]
    tile, wide = tile_of(half, TILE), tile_of(depth, WIDE)
    tiles, pieces = half // tile, depth // wide
    small = 16
    row, col = lax.axis_index("row"), lax.axis_index("col")
    at, side = lax.div(col, PAIR), lax.rem(col, PAIR)
    group, sib = lax.div(at, PAIR), lax.rem(at, PAIR)
    across, core = lax.div(row, PAIR), lax.rem(row, PAIR)
    mate = (across * PAIR + 1 - core, col)
    twin = (row, at * PAIR + 1 - side)

    def on_line(place):
        return (row, place * PAIR + side)

    def on_chip(place):
        return (place * PAIR + core, col)

    beside = group * PAIR + 1 - sib
    sibling = on_line(beside)

    def remote(src, dst, send, recv, device):
        return pltpu.make_async_remote_copy(
            src_ref=src, dst_ref=dst, send_sem=send, recv_sem=recv,
            device_id=device, device_id_type=MESH,
        )

    def group_of(k):
        low = jnp.minimum(group, groups - 1 - group)
        step = lax.div(k + 1, 2)
        near = jnp.where(lax.rem(k, 2) == 1, group + step, group - step)
        far = jnp.where(group < groups - 1 - group, group + (k - low), group - (k - low))
        return jnp.where(k <= 2 * low, near, far)

    def block_of(g, i):
        first = jnp.where(g == group, sib, jnp.where(g > group, 0, 1))
        return g * PAIR + (first if i == 0 else 1 - first)

    def slot(q, s):
        return xs_all.at[block(q * PAIR + s, own), :]

    def slot_half(q, s, h):
        return xs_all.at[block((q * PAIR + s) * 2 + h, own // 2), :]

    def own_to(which, device):
        return remote(x_ref, slot(at, side), z_send.at[which, at], z_recv.at[at], device)

    def own_half(h):
        return remote(
            x_ref.at[block(h, own // 2), :], slot_half(at, side, h),
            y_send.at[at, h], y_recv.at[at, h], twin,
        )

    def to_twin(q, h):
        view = slot_half(q, side, h)
        return remote(view, view, y_send.at[q, h], y_recv.at[q, h], twin)

    def twin_to_sibling():
        view = slot_half(at, 1 - side, 1)
        return remote(view, view, y_send.at[beside, 1], y_recv.at[at, 1], sibling)

    def onward(q):
        place = jnp.clip(jnp.where(q < at, at + 1, at - 1), 0, line - 1)
        return remote(slot(q, side), slot(q, side), z_send.at[1, q], z_recv.at[q], on_line(place))

    def goes_on(q):
        return ((q < at) & (at + 1 < line)) | ((q > at) & (at > 0))

    def wait_z(q):
        remote(slot(q, side), slot(q, side), z_send.at[1, q], z_recv.at[q], twin).wait_recv()

    def wait_y(q, h):
        view = slot_half(q, 1 - side, h)
        remote(view, view, y_send.at[q, h], y_recv.at[q, h], twin).wait_recv()

    def go_copy(step):
        other = lax.rem(row + step, n_row)
        return remote(
            go_ref.at[:, block(lax.rem(other, PAIR), half)],
            go_all.at[block(row, held), :],
            go_send.at[step - 1], go_recv.at[row], (other, col),
        )

    def go_arrived(source):
        view = go_all.at[block(source, held), :]
        return remote(view, view, go_send.at[0], go_recv.at[source], mate)

    def core_copy(g, j):
        return remote(
            part.at[g, :, block((1 - core) * tiles + j, tile)], core_in.at[g, :, block(j, tile)],
            core_send.at[g, j], core_recv.at[g, j], mate,
        )

    def chip_copy(g, step, j):
        place = lax.rem(across + step, chips)
        return remote(
            chip.at[g, :, block(j, tile)], chip_in.at[g, across, :, block(j, tile)],
            chip_send.at[g, step - 1, j], chip_recv.at[g, across, j], on_chip(place),
        )

    def chip_arrived(g, source, j):
        view = chip_in.at[g, source, :, block(j, tile)]
        return remote(view, view, chip_send.at[g, 0, j], chip_recv.at[g, source, j], mate)

    def gp_copy(g, which, j):
        view = gp.at[block(g, big), block(which * tiles + j, tile)]
        return remote(view, view, gp_send.at[g, j], gp_recv.at[g, j], mate)

    def swapped(j):
        return lax.rem(j, 4) == 0

    def by(j, kept, other):
        return jnp.where(swapped(j), other, kept)

    beside_col, twin_col = beside * PAIR + side, at * PAIR + 1 - side

    def pair_copy(g, b, j):
        source = by(j, b * PAIR + 1 - side, (1 - sib) * PAIR + b)
        return remote(
            term.at[g, block(source, own), block(j, wide)],
            pair_in.at[g, block(b, own), block(j, wide)],
            pair_send.at[g, b, j], pair_recv.at[g, b, j], (row, by(j, twin_col, beside_col)),
        )

    def sib_copy(g, j):
        source = by(j, 1 - sib, 1 - side)
        return remote(
            both.at[g, block(source, own), block(j, wide)], sib_in.at[g, :, block(j, wide)],
            sib_send.at[g, j], sib_recv.at[g, j], (row, by(j, beside_col, twin_col)),
        )

    def line_copy(g, j):
        return remote(
            summed.at[g, :, block(j, wide)], line_in.at[group, :, block(j, wide)],
            line_send.at[g, j], line_recv.at[group, j], on_line(g * PAIR + sib),
        )

    def line_arrived(source, j):
        view = line_in.at[source, :, block(j, wide)]
        return remote(view, view, line_send.at[source, j], line_recv.at[source, j], twin)

    def x_copy_out(g):
        return pltpu.make_async_copy(
            xs_all.at[block(g, big), :], x_out.at[block(g, big), :], out_sem.at[0, g]
        )

    def gp_copy_out(g):
        return pltpu.make_async_copy(
            gp.at[block(g, big), :], gp_out.at[block(g, big), :], out_sem.at[1, g]
        )

    w_copy = pltpu.make_async_copy(w_ref, w, w_sem)
    x_copy = pltpu.make_async_copy(x_ref, slot(at, side), x_sem)
    go_own = pltpu.make_async_copy(
        go_ref.at[:, block(core, half)], go_all.at[block(row, held), :], go_sem
    )
    x_copy.start()
    go_own.start()
    w_copy.start()

    barrier = pltpu.get_barrier_semaphore()
    pl.semaphore_signal(barrier, inc=1, device_id=twin, device_id_type=MESH)

    @pl.loop(1, line)
    def _(step):
        pl.semaphore_signal(
            barrier, inc=1, device_id=on_line(lax.rem(at + step, line)), device_id_type=MESH
        )

    @pl.loop(1, n_row)
    def _(step):
        pl.semaphore_signal(
            barrier, inc=1, device_id=(lax.rem(row + step, n_row), col), device_id_type=MESH
        )

    pl.semaphore_wait(barrier, line + n_row - 1)

    up, down = jnp.minimum(at + 1, line - 1), jnp.maximum(at - 1, 0)
    own_half(1).start()

    @pl.when(at + 1 < line)
    def _():
        own_to(1, on_line(up)).start()

    @pl.when(at > 0)
    def _():
        own_to(2, on_line(down)).start()

    own_half(0).start()

    @pl.loop(1, n_row)
    def _(step):
        go_copy(step).start()

    x_copy.wait()
    wait_y(at, 1)
    twin_to_sibling().start()
    wait_z(beside)
    to_twin(beside, 0).start()

    @pl.when(goes_on(beside))
    def _():
        onward(beside).start()

    wait_y(at, 0)

    def slabs(height, base, width, body):
        @pl.loop(0, height // small)
        def _(i):
            body(pl.multiple_of(i * small, small), pl.ds(pl.multiple_of(base * width, width), width))

    def at_row(start):
        return pl.ds(pl.multiple_of(start, small), small)

    def product(g, which):
        columns = block(which, tile)
        part[g, :, columns] = jnp.dot(
            xs_all[block(g, big), :], w[:, columns], preferred_element_type=jnp.float32
        ).astype(part.dtype)

    @pl.loop(0, groups + 3)
    def _(k):
        g = group_of(jnp.minimum(k, groups - 1))
        g1 = group_of(jnp.clip(k - 1, 0, groups - 1))
        g2 = group_of(jnp.clip(k - 2, 0, groups - 1))
        g3 = group_of(jnp.clip(k - 3, 0, groups - 1))
        coming = group_of(jnp.minimum(k + 1, groups - 1))
        more = k + 1 < groups
        first, second = block_of(coming, 0), block_of(coming, 1)

        @pl.when(more & goes_on(first))
        def _():
            wait_z(first)
            onward(first).start()

        @pl.when(k < groups)
        def _():
            for i in range(PAIR):
                @pl.when((k > 0) | (block_of(g, i) != at))
                def _():
                    for h in range(2):
                        wait_y(block_of(g, i), h)

            @pl.when(more & goes_on(first))
            def _():
                for h in range(2):
                    to_twin(first, h).start()

            x_copy_out(g).start()

            @pl.when(k == 0)
            def _():
                w_copy.wait()

            @pl.loop(0, tiles)
            def _(j):
                product(g, (1 - core) * tiles + j)
                core_copy(g, j).start()
                product(g, core * tiles + j)

                @pl.when(more & (j == 0) & ~goes_on(first))
                def _():
                    wait_z(first)
                    for h in range(2):
                        to_twin(first, h).start()

                @pl.when(more & (j == tiles // 2) & goes_on(second))
                def _():
                    wait_z(second)
                    onward(second).start()
                    for h in range(2):
                        to_twin(second, h).start()

                core_copy(g, j).wait_recv()

                def add(top, columns):
                    mine = part[g, at_row(top), block(core * tiles + j, tile)]
                    chip[g, at_row(top), columns] = (
                        mine.astype(jnp.float32)
                        + core_in[g, at_row(top), columns].astype(jnp.float32)
                    ).astype(chip.dtype)

                slabs(big, j, tile, add)

                @pl.loop(1, chips)
                def _(step):
                    chip_copy(g, step, j).start()

            @pl.when(more & ~goes_on(second))
            def _():
                wait_z(second)
                for h in range(2):
                    to_twin(second, h).start()

        @pl.when((k >= 1) & (k <= groups))
        def _():
            @pl.when(k == 1)
            def _():
                go_own.wait()

                @pl.loop(1, n_row)
                def _(step):
                    go_arrived(lax.rem(row + step, n_row)).wait_recv()

            @pl.loop(0, tiles)
            def _(j):
                @pl.loop(1, chips)
                def _(step):
                    chip_arrived(g1, lax.rem(across + step, chips), j).wait_recv()

                def slope(top, columns):
                    total = chip[g1, at_row(top), columns].astype(jnp.float32)
                    for step in range(1, chips):
                        source = lax.rem(across + step, chips)
                        total = total + chip_in[g1, source, at_row(top), columns].astype(jnp.float32)
                    token = at_row(g1 * big + top)
                    gp[token, block(core * tiles + j, tile)] = (
                        go_all[token, columns].astype(jnp.float32) * gelu_slope(total)
                    ).astype(gp.dtype)

                slabs(big, j, tile, slope)
                gp_copy(g1, core, j).start()

            @pl.loop(0, tiles)
            def _(j):
                gp_copy(g1, 1 - core, j).wait_recv()

            gp_copy_out(g1).start()

            @pl.loop(0, pieces)
            def _(j):
                columns = block(j, wide)
                term[g1, :, columns] = lax.dot_general(
                    gp[block(g1, big), :], w[columns, :], (((1,), (1,)), ((), ())),
                    preferred_element_type=jnp.float32,
                ).astype(term.dtype)
                for b in range(PAIR):
                    pair_copy(g1, b, j).start()

        @pl.when((k >= 2) & (k <= groups + 1))
        def _():
            @pl.loop(0, pieces)
            def _(j):
                for b in range(PAIR):
                    pair_copy(g2, b, j).wait_recv()

                    def add(top, columns):
                        mine = term[g2, at_row(by(j, b * PAIR + side, sib * PAIR + b) * own + top), columns]
                        here = at_row(b * own + top)
                        both[g2, here, columns] = (
                            mine.astype(jnp.float32)
                            + pair_in[g2, here, columns].astype(jnp.float32)
                        ).astype(both.dtype)

                    slabs(own, j, wide, add)
                sib_copy(g2, j).start()

        @pl.when(k >= 3)
        def _():
            @pl.loop(0, pieces)
            def _(j):
                sib_copy(g3, j).wait_recv()

                def add(top, columns):
                    mine = both[g3, at_row(by(j, sib, side) * own + top), columns]
                    summed[g3, at_row(top), columns] = (
                        mine.astype(jnp.float32)
                        + sib_in[g3, at_row(top), columns].astype(jnp.float32)
                    ).astype(summed.dtype)

                slabs(own, j, wide, add)

                @pl.when(g3 != group)
                def _():
                    line_copy(g3, j).start()

    @pl.loop(0, pieces)
    def _(j):
        @pl.loop(1, groups)
        def _(step):
            line_arrived(lax.rem(group + step, groups), j).wait_recv()

        def finish(top, columns):
            total = summed[group, at_row(top), columns].astype(jnp.float32)
            for step in range(1, groups):
                source = lax.rem(group + step, groups)
                total = total + line_in[source, at_row(top), columns].astype(jnp.float32)
            gi_ref[at_row(top), columns] = total.astype(gi_ref.dtype)

        slabs(own, j, wide, finish)

    own_half(0).wait_send()
    own_half(1).wait_send()
    twin_to_sibling().wait_send()

    @pl.when(at + 1 < line)
    def _():
        own_to(1, on_line(up)).wait_send()

    @pl.when(at > 0)
    def _():
        own_to(2, on_line(down)).wait_send()

    @pl.loop(1, n_row)
    def _(step):
        go_copy(step).wait_send()

    @pl.loop(0, line)
    def _(q):
        @pl.when(q != at)
        def _():
            to_twin(q, 0).wait_send()

        @pl.when((q != at) & (q != beside))
        def _():
            to_twin(q, 1).wait_send()

        @pl.when(goes_on(q))
        def _():
            onward(q).wait_send()

    @pl.loop(0, groups)
    def _(g):
        @pl.loop(0, tiles)
        def _(j):
            core_copy(g, j).wait_send()

            @pl.loop(1, chips)
            def _(step):
                chip_copy(g, step, j).wait_send()

            gp_copy(g, core, j).wait_send()

        @pl.loop(0, pieces)
        def _(j):
            for b in range(PAIR):
                pair_copy(g, b, j).wait_send()
            sib_copy(g, j).wait_send()

            @pl.when(g != group)
            def _():
                line_copy(g, j).wait_send()

        x_copy_out(g).wait()
        gp_copy_out(g).wait()


def fused(n_row, n_col, inputs, weight, grad_out):
    own, depth = inputs.shape
    units = weight.shape[1]
    half = units // PAIR
    line, chips = n_col // PAIR, n_row // PAIR
    groups = line // PAIR
    big, tokens = own * PAIR * PAIR, own * n_col
    tiles, pieces = half // tile_of(half, TILE), depth // tile_of(depth, WIDE)
    held = grad_out.shape[0]
    bf16 = jnp.bfloat16
    DMA = pltpu.SemaphoreType.DMA
    flops = 4 * tokens * depth * units
    return pl.pallas_call(
        functools.partial(kernel, n_row, n_col),
        out_shape=(
            jax.ShapeDtypeStruct((own, depth), bf16),
            jax.ShapeDtypeStruct((tokens, depth), bf16),
            jax.ShapeDtypeStruct((tokens, units), bf16),
        ),
        in_specs=[pl.BlockSpec(memory_space=pl.ANY)] * 3,
        out_specs=(
            pl.BlockSpec(memory_space=pltpu.VMEM),
            pl.BlockSpec(memory_space=pl.ANY),
            pl.BlockSpec(memory_space=pl.ANY),
        ),
        scratch_shapes=[
            pltpu.VMEM((depth, units), bf16),
            pltpu.VMEM((tokens, depth), bf16),
            pltpu.VMEM((held * n_row, half), bf16),
            pltpu.VMEM((groups, big, units), bf16),
            pltpu.VMEM((groups, big, half), bf16),
            pltpu.VMEM((groups, big, half), bf16),
            pltpu.VMEM((groups, chips, big, half), bf16),
            pltpu.VMEM((tokens, units), bf16),
            pltpu.VMEM((groups, big, depth), bf16),
            pltpu.VMEM((groups, own * PAIR, depth), bf16),
            pltpu.VMEM((groups, own * PAIR, depth), bf16),
            pltpu.VMEM((groups, own, depth), bf16),
            pltpu.VMEM((groups, own, depth), bf16),
            pltpu.VMEM((groups, own, depth), bf16),
            DMA, DMA, DMA, DMA((2, groups)),
            DMA((line,)), DMA((3, line)), DMA((line, 2)), DMA((line, 2)),
            DMA((n_row,)), DMA((n_row,)),
            DMA((groups, tiles)), DMA((groups, tiles)),
            DMA((groups, chips, tiles)), DMA((groups, chips, tiles)),
            DMA((groups, tiles)), DMA((groups, tiles)),
            DMA((groups, PAIR, pieces)), DMA((groups, PAIR, pieces)),
            DMA((groups, pieces)), DMA((groups, pieces)),
            DMA((groups, pieces)), DMA((groups, pieces)),
        ],
        cost_estimate=pl.CostEstimate(
            flops=flops, bytes_accessed=2 * depth * units, transcendentals=tokens * half
        ),
        compiler_params=pltpu.CompilerParams(
            collective_id=0, has_side_effects=True, vmem_limit_bytes=58 * 1024 * 1024
        ),
    )(inputs, weight, grad_out)


def weight_kernel(x_ref, gp_ref, gw_ref, turned):
    turned[...] = x_ref[...].T
    width = tile_of(gp_ref.shape[1], 1024)

    @pl.loop(0, gp_ref.shape[1] // width)
    def _(j):
        columns = block(j, width)
        gw_ref[:, columns] = jnp.dot(
            turned[...], gp_ref[:, columns], preferred_element_type=jnp.float32
        ).astype(gw_ref.dtype)


def weight_gradient(gathered, grad_pre):
    tokens, depth = gathered.shape
    units = grad_pre.shape[1]
    high = tile_of(depth, 512)
    return pl.pallas_call(
        weight_kernel,
        out_shape=jax.ShapeDtypeStruct((depth, units), jnp.bfloat16),
        grid=(depth // high,),
        in_specs=[
            pl.BlockSpec((tokens, high), lambda i: (0, i)),
            pl.BlockSpec((tokens, units), lambda i: (0, 0)),
        ],
        out_specs=pl.BlockSpec((high, units), lambda i: (i, 0)),
        scratch_shapes=[pltpu.VMEM((high, tokens), jnp.bfloat16)],
        cost_estimate=pl.CostEstimate(
            flops=2 * tokens * depth * units,
            bytes_accessed=2 * (depth * units + tokens * depth + tokens * units),
            transcendentals=0,
        ),
        compiler_params=pltpu.CompilerParams(vmem_limit_bytes=48 * 1024 * 1024),
    )(gathered, grad_pre)


def solution(mesh):
    n_row, n_col = mesh.shape["row"], mesh.shape["col"]

    def shards(inputs, weight, grad_out):
        grad_input, gathered, grad_pre = fused(n_row, n_col, inputs, weight, grad_out)
        return grad_input, weight_gradient(gathered, grad_pre)

    return jax.shard_map(
        shards,
        mesh=mesh,
        in_specs=(P("col", "row"), P("row", "col"), P("row", "col")),
        out_specs=(P("col", "row"), P("row", "col")),
        check_vma=False,
    )
```

```python
import functools

import jax
import jax.numpy as jnp
from jax import lax
from jax.experimental import pallas as pl
from jax.experimental.pallas import tpu as pltpu
from jax.sharding import PartitionSpec as P

MESH = pl.DeviceIdType.MESH
PAIR = 2
TILE = 512
WIDE = 768


def gelu_slope(value):
    coef = 0.7978845608
    inner = coef * (value + 0.044715 * value * value * value)
    tanh_val = jnp.tanh(inner)
    return 0.5 * (1.0 + tanh_val) + 0.5 * value * (1.0 - tanh_val * tanh_val) * coef * (
        1.0 + 3.0 * 0.044715 * value * value
    )


def tile_of(width, most):
    tile = 128
    for size in range(128, most + 1, 128):
        if width % size == 0:
            tile = size
    return tile


def block(index, size):
    return pl.ds(pl.multiple_of(index * size, size), size)


def kernel(
    n_row, n_col,
    x_ref, w_ref, go_ref,
    gi_ref, x_out, gp_out,
    w, xs_all, go_all, part, core_in, chip, chip_in, gp, term, pair_in, both, sib_in, summed, line_in,
    w_sem, x_sem, go_sem, out_sem,
    z_recv, z_send, y_recv, y_send, go_recv, go_send, core_recv, core_send, chip_recv, chip_send,
    gp_recv, gp_send, pair_recv, pair_send, sib_recv, sib_send, line_recv, line_send,
):
    own, depth = x_ref.shape
    units = w_ref.shape[1]
    half = units // PAIR
    line = n_col // PAIR
    groups = line // PAIR
    chips = n_row // PAIR
    big = own * PAIR * PAIR
    held = go_ref.shape[0]
    tile, wide = tile_of(half, TILE), tile_of(depth, WIDE)
    tiles, pieces = half // tile, depth // wide
    small = 16
    row, col = lax.axis_index("row"), lax.axis_index("col")
    at, side = lax.div(col, PAIR), lax.rem(col, PAIR)
    group, sib = lax.div(at, PAIR), lax.rem(at, PAIR)
    across, core = lax.div(row, PAIR), lax.rem(row, PAIR)
    mate = (across * PAIR + 1 - core, col)
    twin = (row, at * PAIR + 1 - side)

    def on_line(place):
        return (row, place * PAIR + side)

    def on_chip(place):
        return (place * PAIR + core, col)

    beside = group * PAIR + 1 - sib
    sibling = on_line(beside)

    def remote(src, dst, send, recv, device):
        return pltpu.make_async_remote_copy(
            src_ref=src, dst_ref=dst, send_sem=send, recv_sem=recv,
            device_id=device, device_id_type=MESH,
        )

    def group_of(k):
        low = jnp.minimum(group, groups - 1 - group)
        step = lax.div(k + 1, 2)
        near = jnp.where(lax.rem(k, 2) == 1, group + step, group - step)
        far = jnp.where(group < groups - 1 - group, group + (k - low), group - (k - low))
        return jnp.where(k <= 2 * low, near, far)

    def block_of(g, i):
        first = jnp.where(g == group, sib, jnp.where(g > group, 0, 1))
        return g * PAIR + (first if i == 0 else 1 - first)

    def slot(q, s):
        return xs_all.at[block(q * PAIR + s, own), :]

    def slot_half(q, s, h):
        return xs_all.at[block((q * PAIR + s) * 2 + h, own // 2), :]

    def own_to(which, device):
        return remote(x_ref, slot(at, side), z_send.at[which, at], z_recv.at[at], device)

    def own_half(h):
        return remote(
            x_ref.at[block(h, own // 2), :], slot_half(at, side, h),
            y_send.at[at, h], y_recv.at[at, h], twin,
        )

    def to_twin(q, h):
        view = slot_half(q, side, h)
        return remote(view, view, y_send.at[q, h], y_recv.at[q, h], twin)

    def twin_to_sibling():
        view = slot_half(at, 1 - side, 1)
        return remote(view, view, y_send.at[beside, 1], y_recv.at[at, 1], sibling)

    def onward(q):
        place = jnp.clip(jnp.where(q < at, at + 1, at - 1), 0, line - 1)
        return remote(slot(q, side), slot(q, side), z_send.at[1, q], z_recv.at[q], on_line(place))

    def goes_on(q):
        return ((q < at) & (at + 1 < line)) | ((q > at) & (at > 0))

    def wait_z(q):
        remote(slot(q, side), slot(q, side), z_send.at[1, q], z_recv.at[q], twin).wait_recv()

    def wait_y(q, h):
        view = slot_half(q, 1 - side, h)
        remote(view, view, y_send.at[q, h], y_recv.at[q, h], twin).wait_recv()

    def go_copy(step):
        other = lax.rem(row + step, n_row)
        return remote(
            go_ref.at[:, block(lax.rem(other, PAIR), half)],
            go_all.at[block(row, held), :],
            go_send.at[step - 1], go_recv.at[row], (other, col),
        )

    def go_arrived(source):
        view = go_all.at[block(source, held), :]
        return remote(view, view, go_send.at[0], go_recv.at[source], mate)

    def core_copy(g, j):
        return remote(
            part.at[g, :, block((1 - core) * tiles + j, tile)], core_in.at[g, :, block(j, tile)],
            core_send.at[g, j], core_recv.at[g, j], mate,
        )

    def chip_copy(g, step, j):
        place = lax.rem(across + step, chips)
        return remote(
            chip.at[g, :, block(j, tile)], chip_in.at[g, across, :, block(j, tile)],
            chip_send.at[g, step - 1, j], chip_recv.at[g, across, j], on_chip(place),
        )

    def chip_arrived(g, source, j):
        view = chip_in.at[g, source, :, block(j, tile)]
        return remote(view, view, chip_send.at[g, 0, j], chip_recv.at[g, source, j], mate)

    def gp_copy(g, which, j):
        view = gp.at[block(g, big), block(which * tiles + j, tile)]
        return remote(view, view, gp_send.at[g, j], gp_recv.at[g, j], mate)

    def swapped(j):
        return lax.rem(j, 4) == 0

    def by(j, kept, other):
        return jnp.where(swapped(j), other, kept)

    beside_col, twin_col = beside * PAIR + side, at * PAIR + 1 - side

    def pair_copy(g, b, j):
        source = by(j, b * PAIR + 1 - side, (1 - sib) * PAIR + b)
        return remote(
            term.at[g, block(source, own), block(j, wide)],
            pair_in.at[g, block(b, own), block(j, wide)],
            pair_send.at[g, b, j], pair_recv.at[g, b, j], (row, by(j, twin_col, beside_col)),
        )

    def sib_copy(g, j):
        source = by(j, 1 - sib, 1 - side)
        return remote(
            both.at[g, block(source, own), block(j, wide)], sib_in.at[g, :, block(j, wide)],
            sib_send.at[g, j], sib_recv.at[g, j], (row, by(j, beside_col, twin_col)),
        )

    def line_copy(g, j):
        return remote(
            summed.at[g, :, block(j, wide)], line_in.at[group, :, block(j, wide)],
            line_send.at[g, j], line_recv.at[group, j], on_line(g * PAIR + sib),
        )

    def line_arrived(source, j):
        view = line_in.at[source, :, block(j, wide)]
        return remote(view, view, line_send.at[source, j], line_recv.at[source, j], twin)

    def x_copy_out(g):
        return pltpu.make_async_copy(
            xs_all.at[block(g, big), :], x_out.at[block(g, big), :], out_sem.at[0, g]
        )

    def gp_copy_out(g):
        return pltpu.make_async_copy(
            gp.at[block(g, big), :], gp_out.at[block(g, big), :], out_sem.at[1, g]
        )

    w_copy = pltpu.make_async_copy(w_ref, w, w_sem)
    x_copy = pltpu.make_async_copy(x_ref, slot(at, side), x_sem)
    go_own = pltpu.make_async_copy(
        go_ref.at[:, block(core, half)], go_all.at[block(row, held), :], go_sem
    )
    x_copy.start()
    go_own.start()
    w_copy.start()

    barrier = pltpu.get_barrier_semaphore()
    pl.semaphore_signal(barrier, inc=1, device_id=twin, device_id_type=MESH)

    @pl.loop(1, line)
    def _(step):
        pl.semaphore_signal(
            barrier, inc=1, device_id=on_line(lax.rem(at + step, line)), device_id_type=MESH
        )

    @pl.loop(1, n_row)
    def _(step):
        pl.semaphore_signal(
            barrier, inc=1, device_id=(lax.rem(row + step, n_row), col), device_id_type=MESH
        )

    pl.semaphore_wait(barrier, line + n_row - 1)

    up, down = jnp.minimum(at + 1, line - 1), jnp.maximum(at - 1, 0)
    own_half(1).start()

    @pl.when(at + 1 < line)
    def _():
        own_to(1, on_line(up)).start()

    @pl.when(at > 0)
    def _():
        own_to(2, on_line(down)).start()

    own_half(0).start()

    @pl.loop(1, n_row)
    def _(step):
        go_copy(step).start()

    x_copy.wait()
    wait_y(at, 1)
    twin_to_sibling().start()
    wait_z(beside)
    to_twin(beside, 0).start()

    @pl.when(goes_on(beside))
    def _():
        onward(beside).start()

    wait_y(at, 0)

    def slabs(height, base, width, body):
        @pl.loop(0, height // small)
        def _(i):
            body(pl.multiple_of(i * small, small), pl.ds(pl.multiple_of(base * width, width), width))

    def at_row(start):
        return pl.ds(pl.multiple_of(start, small), small)

    def product(g, which):
        columns = block(which, tile)
        part[g, :, columns] = jnp.dot(
            xs_all[block(g, big), :], w[:, columns], preferred_element_type=jnp.float32
        ).astype(part.dtype)

    @pl.loop(0, groups + 2)
    def _(k):
        g = group_of(jnp.minimum(k, groups - 1))
        g1 = group_of(jnp.clip(k - 1, 0, groups - 1))
        g2 = group_of(jnp.clip(k - 2, 0, groups - 1))
        coming = group_of(jnp.minimum(k + 1, groups - 1))
        more = k + 1 < groups
        first, second = block_of(coming, 0), block_of(coming, 1)

        @pl.when(more & goes_on(first))
        def _():
            wait_z(first)
            onward(first).start()

        @pl.when(k < groups)
        def _():
            for i in range(PAIR):
                @pl.when((k > 0) | (block_of(g, i) != at))
                def _():
                    for h in range(2):
                        wait_y(block_of(g, i), h)

            @pl.when(more & goes_on(first))
            def _():
                for h in range(2):
                    to_twin(first, h).start()

            x_copy_out(g).start()

            @pl.when(k == 0)
            def _():
                w_copy.wait()

            @pl.loop(0, tiles)
            def _(j):
                product(g, (1 - core) * tiles + j)
                core_copy(g, j).start()
                product(g, core * tiles + j)

                @pl.when(more & (j == 0) & ~goes_on(first))
                def _():
                    wait_z(first)
                    for h in range(2):
                        to_twin(first, h).start()

                @pl.when(more & (j == tiles // 2) & goes_on(second))
                def _():
                    wait_z(second)
                    onward(second).start()
                    for h in range(2):
                        to_twin(second, h).start()

                core_copy(g, j).wait_recv()

                def add(top, columns):
                    mine = part[g, at_row(top), block(core * tiles + j, tile)]
                    chip[g, at_row(top), columns] = (
                        mine.astype(jnp.float32)
                        + core_in[g, at_row(top), columns].astype(jnp.float32)
                    ).astype(chip.dtype)

                slabs(big, j, tile, add)

                @pl.loop(1, chips)
                def _(step):
                    chip_copy(g, step, j).start()

            @pl.when(more & ~goes_on(second))
            def _():
                wait_z(second)
                for h in range(2):
                    to_twin(second, h).start()

        @pl.when((k >= 1) & (k <= groups))
        def _():
            @pl.when(k == 1)
            def _():
                go_own.wait()

                @pl.loop(1, n_row)
                def _(step):
                    go_arrived(lax.rem(row + step, n_row)).wait_recv()

            @pl.loop(0, tiles)
            def _(j):
                @pl.loop(1, chips)
                def _(step):
                    chip_arrived(g1, lax.rem(across + step, chips), j).wait_recv()

                def slope(top, columns):
                    total = chip[g1, at_row(top), columns].astype(jnp.float32)
                    for step in range(1, chips):
                        source = lax.rem(across + step, chips)
                        total = total + chip_in[g1, source, at_row(top), columns].astype(jnp.float32)
                    token = at_row(g1 * big + top)
                    gp[token, block(core * tiles + j, tile)] = (
                        go_all[token, columns].astype(jnp.float32) * gelu_slope(total)
                    ).astype(gp.dtype)

                slabs(big, j, tile, slope)
                gp_copy(g1, core, j).start()

            @pl.loop(0, tiles)
            def _(j):
                gp_copy(g1, 1 - core, j).wait_recv()

            gp_copy_out(g1).start()

            @pl.loop(0, pieces)
            def _(j):
                columns = block(j, wide)
                term[g1, :, columns] = lax.dot_general(
                    gp[block(g1, big), :], w[columns, :], (((1,), (1,)), ((), ())),
                    preferred_element_type=jnp.float32,
                ).astype(term.dtype)
                for b in range(PAIR):
                    pair_copy(g1, b, j).start()

        @pl.when(k >= 2)
        def _():
            @pl.loop(0, pieces + 1)
            def _(step):
                @pl.when(step < pieces)
                def _():
                    j = jnp.minimum(step, pieces - 1)
                    for b in range(PAIR):
                        pair_copy(g2, b, j).wait_recv()

                        def add(top, columns):
                            start = by(j, b * PAIR + side, sib * PAIR + b) * own
                            mine = term[g2, at_row(start + top), columns]
                            here = at_row(b * own + top)
                            both[g2, here, columns] = (
                                mine.astype(jnp.float32)
                                + pair_in[g2, here, columns].astype(jnp.float32)
                            ).astype(both.dtype)

                        slabs(own, j, wide, add)
                    sib_copy(g2, j).start()

                @pl.when(step >= 1)
                def _():
                    j = jnp.maximum(step - 1, 0)
                    sib_copy(g2, j).wait_recv()

                    def add(top, columns):
                        mine = both[g2, at_row(by(j, sib, side) * own + top), columns]
                        summed[g2, at_row(top), columns] = (
                            mine.astype(jnp.float32)
                            + sib_in[g2, at_row(top), columns].astype(jnp.float32)
                        ).astype(summed.dtype)

                    slabs(own, j, wide, add)

                    @pl.when(g2 != group)
                    def _():
                        line_copy(g2, j).start()

    @pl.loop(0, pieces)
    def _(j):
        @pl.loop(1, groups)
        def _(step):
            line_arrived(lax.rem(group + step, groups), j).wait_recv()

        def finish(top, columns):
            total = summed[group, at_row(top), columns].astype(jnp.float32)
            for step in range(1, groups):
                source = lax.rem(group + step, groups)
                total = total + line_in[source, at_row(top), columns].astype(jnp.float32)
            gi_ref[at_row(top), columns] = total.astype(gi_ref.dtype)

        slabs(own, j, wide, finish)

    own_half(0).wait_send()
    own_half(1).wait_send()
    twin_to_sibling().wait_send()

    @pl.when(at + 1 < line)
    def _():
        own_to(1, on_line(up)).wait_send()

    @pl.when(at > 0)
    def _():
        own_to(2, on_line(down)).wait_send()

    @pl.loop(1, n_row)
    def _(step):
        go_copy(step).wait_send()

    @pl.loop(0, line)
    def _(q):
        @pl.when(q != at)
        def _():
            to_twin(q, 0).wait_send()

        @pl.when((q != at) & (q != beside))
        def _():
            to_twin(q, 1).wait_send()

        @pl.when(goes_on(q))
        def _():
            onward(q).wait_send()

    @pl.loop(0, groups)
    def _(g):
        @pl.loop(0, tiles)
        def _(j):
            core_copy(g, j).wait_send()

            @pl.loop(1, chips)
            def _(step):
                chip_copy(g, step, j).wait_send()

            gp_copy(g, core, j).wait_send()

        @pl.loop(0, pieces)
        def _(j):
            for b in range(PAIR):
                pair_copy(g, b, j).wait_send()
            sib_copy(g, j).wait_send()

            @pl.when(g != group)
            def _():
                line_copy(g, j).wait_send()

        x_copy_out(g).wait()
        gp_copy_out(g).wait()


def fused(n_row, n_col, inputs, weight, grad_out):
    own, depth = inputs.shape
    units = weight.shape[1]
    half = units // PAIR
    line, chips = n_col // PAIR, n_row // PAIR
    groups = line // PAIR
    big, tokens = own * PAIR * PAIR, own * n_col
    tiles, pieces = half // tile_of(half, TILE), depth // tile_of(depth, WIDE)
    held = grad_out.shape[0]
    bf16 = jnp.bfloat16
    DMA = pltpu.SemaphoreType.DMA
    flops = 4 * tokens * depth * units
    return pl.pallas_call(
        functools.partial(kernel, n_row, n_col),
        out_shape=(
            jax.ShapeDtypeStruct((own, depth), bf16),
            jax.ShapeDtypeStruct((tokens, depth), bf16),
            jax.ShapeDtypeStruct((tokens, units), bf16),
        ),
        in_specs=[pl.BlockSpec(memory_space=pl.ANY)] * 3,
        out_specs=(
            pl.BlockSpec(memory_space=pltpu.VMEM),
            pl.BlockSpec(memory_space=pl.ANY),
            pl.BlockSpec(memory_space=pl.ANY),
        ),
        scratch_shapes=[
            pltpu.VMEM((depth, units), bf16),
            pltpu.VMEM((tokens, depth), bf16),
            pltpu.VMEM((held * n_row, half), bf16),
            pltpu.VMEM((groups, big, units), bf16),
            pltpu.VMEM((groups, big, half), bf16),
            pltpu.VMEM((groups, big, half), bf16),
            pltpu.VMEM((groups, chips, big, half), bf16),
            pltpu.VMEM((tokens, units), bf16),
            pltpu.VMEM((groups, big, depth), bf16),
            pltpu.VMEM((groups, own * PAIR, depth), bf16),
            pltpu.VMEM((groups, own * PAIR, depth), bf16),
            pltpu.VMEM((groups, own, depth), bf16),
            pltpu.VMEM((groups, own, depth), bf16),
            pltpu.VMEM((groups, own, depth), bf16),
            DMA, DMA, DMA, DMA((2, groups)),
            DMA((line,)), DMA((3, line)), DMA((line, 2)), DMA((line, 2)),
            DMA((n_row,)), DMA((n_row,)),
            DMA((groups, tiles)), DMA((groups, tiles)),
            DMA((groups, chips, tiles)), DMA((groups, chips, tiles)),
            DMA((groups, tiles)), DMA((groups, tiles)),
            DMA((groups, PAIR, pieces)), DMA((groups, PAIR, pieces)),
            DMA((groups, pieces)), DMA((groups, pieces)),
            DMA((groups, pieces)), DMA((groups, pieces)),
        ],
        cost_estimate=pl.CostEstimate(
            flops=flops, bytes_accessed=2 * depth * units, transcendentals=tokens * half
        ),
        compiler_params=pltpu.CompilerParams(
            collective_id=0, has_side_effects=True, vmem_limit_bytes=58 * 1024 * 1024
        ),
    )(inputs, weight, grad_out)


def solution(mesh):
    n_row, n_col = mesh.shape["row"], mesh.shape["col"]

    def shards(inputs, weight, grad_out):
        grad_input, gathered, grad_pre = fused(n_row, n_col, inputs, weight, grad_out)
        grad_weight = lax.dot_general(
            gathered, grad_pre, (((0,), (0,)), ((), ())), preferred_element_type=jnp.float32
        )
        return grad_input, grad_weight.astype(jnp.bfloat16)

    return jax.shard_map(
        shards,
        mesh=mesh,
        in_specs=(P("col", "row"), P("row", "col"), P("row", "col")),
        out_specs=(P("col", "row"), P("row", "col")),
        check_vma=False,
    )
```
